1024 devices in a mesh: row: 8 (over x, core), col: 128 (over z, y).
Axes of the slice: x: 4, y: 8, z: 16, core: 2. Of those that a mesh axis runs over, the one named last changes fastest.
Arguments:
- vectors: float32 [16384, 16384], P('row', 'col'), may hold values from -6 to 6
- reflectors: float32 [8, 256, 256, 128], P('row', 'col'), may hold values from -0.375 to 0.375
- wy_factors: float32 [8, 256, 128, 128], P('row', 'col'), may hold values from -1 to 3, as said below
- block_slots: int32 [8, 4, 4], P('row'), may hold values from 0 to 255, as said below
- offsets: int32 [8, 4, 3], P('row'), may hold values from 0 to 1792
Outputs:
- transformed: float32 [16384, 16384], P('row', 'col')
The draws below stay inside these ranges and needn't reach their ends.
Inputs may be any that keep to these rules, and one draw needn't show every extreme that they name: `wy_factors`: upper triangular; diagonal entries between 1.2 and 2.8. `block_slots`: the entries of one row group are distinct; slot k of every group lies on the col index k // 2. The border entry of the last row group is not read.
All inputs are finite; a program needn't handle non-finite values.
Results may differ from the reference program's by a relative error of at most 0.00026.
Values sent between devices are 32-bit elements; how exact they have to be, the bound alone decides.
A program may use at most 32 MiB of HBM per device.

```python
import jax
import jax.numpy as jnp
from jax import lax

REFLECTOR_WIDTH = 128
REFLECTOR_ROWS = 256
ROWS_DEV = 2048
VEC_DEV = 128
STEPS = 4
BLK = 3
GROUP_SLOTS = 256
NROWS = 16384
NVEC = 16384
N_ROW = 8


def draw_block_slots(key, part):
    used = STEPS * (BLK + 1)
    group_total_count = NROWS // ROWS_DEV
    keys = jax.random.split(key, group_total_count)

    def one_group(group_sort_key, group_no):
        sorted_order = jax.random.permutation(group_sort_key, GROUP_SLOTS)
        top_position = jnp.argmax(sorted_order == GROUP_SLOTS - 1)
        rolled = jnp.roll(sorted_order, -top_position)
        chosen = jnp.where(group_no == 0, rolled, sorted_order)
        return chosen[:used]
    table = jax.vmap(one_group)(keys, jnp.arange(group_total_count))
    return table.reshape(group_total_count, STEPS, BLK + 1).astype(jnp.int32)


def draw_wy_factors(key, part):
    group_total_count = NROWS // ROWS_DEV
    first_key, second_key = jax.random.split(key)
    array_shape = (group_total_count, GROUP_SLOTS, REFLECTOR_WIDTH, REFLECTOR_WIDTH)
    diagonal = jax.random.uniform(first_key, array_shape[:3], jnp.float32, 1.5, 2.5)
    upper = 0.05 * jax.random.normal(second_key, array_shape, jnp.float32)
    strict = jnp.triu(jnp.ones((REFLECTOR_WIDTH, REFLECTOR_WIDTH), jnp.float32), 1)
    return upper * strict + diagonal[..., None] * jnp.eye(REFLECTOR_WIDTH, dtype=jnp.float32)


def plant(drawn, rng, low, largest):
    extent = drawn.shape
    index_at = [jax.random.randint(jax.random.fold_in(rng, axis), (), 0, extent[axis]) for axis in range(len(extent))]
    drawn = drawn.at[tuple(index_at)].set(low)
    longest = extent.index(max(extent))
    index_at[longest] = (index_at[longest] + 1) % extent[longest]
    return drawn.at[tuple(index_at)].set(largest)


def block_scale(rng, shape, cuts, least, largest):
    def one(dim, shards_of):
        heights = jax.random.uniform(jax.random.fold_in(jax.random.fold_in(rng, 6), dim), (shards_of,), jnp.float32, least / len(cuts), largest / len(cuts))
        return jnp.repeat(jnp.exp(heights), shape[dim] // shards_of).reshape((-1,) + (1,) * (len(shape) - dim - 1))

    level = one(*cuts[0])
    for cut in cuts[1:]:
        level = level * one(*cut)
    return level


def scatter_about(own_key, extent, deviation, bound, cuts=(), kind=jnp.bfloat16):
    loudness = block_scale(own_key, extent, cuts, -0.22, 0.18) if cuts else 1.0
    values = jax.random.normal(own_key, extent, jnp.float32) * deviation * loudness
    return jnp.minimum(jnp.maximum(values, -bound), bound).astype(kind)


def setup_inputs(seed: int = 0) -> dict:
    arg_keys = jax.random.split(jax.random.key(seed), 6)
    return {
        "vectors": scatter_about(arg_keys[0], (NROWS, NVEC), 1.0, 6.0, ((0, 8), (1, 128)), jnp.float32),
        "reflectors": scatter_about(arg_keys[1], (N_ROW, GROUP_SLOTS, REFLECTOR_ROWS, REFLECTOR_WIDTH), REFLECTOR_ROWS ** -0.5, 0.375, ((0, 8), (1, 128)), jnp.float32),
        "wy_factors": draw_wy_factors(jax.random.fold_in(arg_keys[5], 71), 0),
        "block_slots": draw_block_slots(jax.random.fold_in(arg_keys[5], 71), 0),
        "offsets": plant(jax.random.randint(arg_keys[4], (N_ROW, STEPS, BLK), 0, ROWS_DEV - REFLECTOR_ROWS + 1), jax.random.fold_in(arg_keys[4], 1), 0, ROWS_DEV - REFLECTOR_ROWS).astype(jnp.int32),
    }


def reflect(block, basis, factor):
    best = lax.Precision.HIGHEST
    coeffs = jnp.dot(basis.T, block, precision=best, preferred_element_type=jnp.float32)
    scaled = jnp.dot(factor, coeffs, precision=best, preferred_element_type=jnp.float32)
    return block - jnp.dot(basis, scaled, precision=best, preferred_element_type=jnp.float32)


def sweep(columns, reflectors, wy_factors, block_slots, offsets):
    group_total_count = NROWS // ROWS_DEV
    current = columns
    for step_no in range(STEPS):
        for group_no in range(group_total_count):
            for block_no in range(BLK + 1):
                if block_no < BLK:
                    start = (group_no * ROWS_DEV + offsets[group_no, step_no, block_no]).astype(jnp.int32)
                elif group_no < group_total_count - 1:
                    start = (group_no + 1) * ROWS_DEV - REFLECTOR_WIDTH
                else:
                    continue
                slot_id = block_slots[group_no, step_no, block_no]
                block = lax.dynamic_slice_in_dim(current, start, REFLECTOR_ROWS, 0)
                block = reflect(block, reflectors[group_no][slot_id], wy_factors[group_no][slot_id])
                current = lax.dynamic_update_slice_in_dim(current, block, start, 0)
    return current


def reference(vectors, reflectors, wy_factors, block_slots, offsets):
    pieces = vectors.reshape(NROWS, NVEC // VEC_DEV, VEC_DEV).transpose(1, 0, 2)
    result = lax.map(lambda column_set: sweep(column_set, reflectors, wy_factors, block_slots, offsets), pieces)
    return result.transpose(1, 0, 2).reshape(NROWS, NVEC)
```

```python
import functools

import jax
import jax.numpy as jnp
from jax import lax
from jax.experimental import pallas as pl
from jax.experimental.pallas import tpu as pltpu
from jax.sharding import PartitionSpec as P

MESH = pl.DeviceIdType.MESH
F32 = jnp.float32
BF16 = jnp.bfloat16
NY = 8
T = 4
PIECES = T * T
REACH = 896

TILE = [(dz, dy) for dz in (-1, 0, 1, 2) for dy in (-1, 0, 1, 2)]
NEAR = [(1, 0), (-1, 0), (2, 0), (-2, 0), (0, 1), (0, -1), (0, 2), (0, -2)]


def split(x):
    high = x.astype(BF16)
    return high, (x - high.astype(F32)).astype(BF16)


def mul(a, b):
    (ah, al), (bh, bl) = a, b
    dot = functools.partial(jnp.dot, preferred_element_type=F32)
    return dot(ah, bh) + (dot(ah, bl) + dot(al, bh))


def kernel(
    nz, groups, steps, inner,
    slots, offs, vec, refl, wy, out,
    got_v, got_t, mine, far, full, ident, shift_x, shift_e, head, beneath, down, delta,
    load_sem, s1, r1, s2, r2, s3, r3, s4, r4, s5, r5, sh, rh,
):
    blocks_step = inner + 1
    blocks = steps * blocks_step
    nzh, nyh = nz // T, NY // T
    nfar = nzh * nyh
    share = blocks // nfar
    group = lax.axis_index("row")
    col = lax.axis_index("col")
    z, y = col // NY, col % NY
    zl, yl, zh, yh = z % T, y % T, z // T, y // T
    f_me = zh * nyh + yh
    p_me = zl * T + yl

    def at(dz, dy):
        return {"col": ((z + dz + nz) % nz) * NY + (y + dy + NY) % NY}

    def row(d):
        return {"row": (group + d + groups) % groups}

    def send(src, dst, ssem, rsem, dev):
        return pltpu.make_async_remote_copy(
            src_ref=src, dst_ref=dst, send_sem=ssem, recv_sem=rsem, device_id=dev, device_id_type=MESH
        )

    fars = [(a, b) for a in range(nzh) for b in range(nyh) if (a, b) != (0, 0)]

    load = pltpu.make_async_copy(vec, out, load_sem.at[0])
    load.start()

    greet = {(-dz, -dy) for dz, dy in TILE} | set(NEAR)
    greet = {(dz % nz, dy % NY) for dz, dy in greet} | {(T * a, T * b) for a, b in fars}
    greet = sorted(greet - {(0, 0)})
    barrier = pltpu.get_barrier_semaphore()
    for dz, dy in greet:
        pl.semaphore_signal(barrier, inc=1, device_id=at(dz, dy), device_id_type=MESH)
    for d in (1, -1):
        pl.semaphore_signal(barrier, inc=1, device_id=row(d), device_id_type=MESH)
    pl.semaphore_wait(barrier, len(greet) + 2)

    first, own = [], []
    vr = got_v.shape[2]
    tr = got_t.shape[2]
    for k, (dz, dy) in enumerate(TILE):
        p = ((z + dz + nz) % T) * T + (y + dy + NY) % T
        src_v = refl.at[0, :, pl.ds(pl.multiple_of(p * vr, vr), vr)]
        src_t = wy.at[0, :, pl.ds(pl.multiple_of(p * tr, tr), tr)]
        if (dz, dy) == (0, 0):
            own = [
                pltpu.make_async_copy(src_v, got_v.at[k], load_sem.at[1]),
                pltpu.make_async_copy(src_t, got_t.at[k], load_sem.at[2]),
            ]
        else:
            first += [
                send(src_v, got_v.at[k], s1.at[k], r1.at[k], at(dz, dy)),
                send(src_t, got_t.at[k], s1.at[k + PIECES], r1.at[k + PIECES], at(dz, dy)),
            ]
    for c in first + own:
        c.start()

    shift_x[...] = jnp.zeros_like(shift_x)
    shift_e[...] = jnp.zeros_like(shift_e)
    for c in own:
        c.wait()
    for c in first:
        c.wait_recv()

    for b in range(blocks):
        slot = slots[0, b // blocks_step, b % blocks_step]
        root = slot // 2
        az = (z - root // NY + nz + 1) % nz
        ay = (y - root % NY + NY + 1) % NY
        here = jnp.logical_and(az < T, ay < T)
        k = jnp.minimum(az, T - 1) * T + jnp.minimum(ay, T - 1)
        half = slot % 2
        mine[b, 0:vr] = jnp.where(here, got_v[k, half], 0.0)
        mine[b, vr : vr + tr] = jnp.where(here, got_t[k, half], 0.0)
    second = []
    for a, b in fars:
        k = a * nyh + b
        dest = ((zh + a) % nzh) * nyh + (yh + b) % nyh
        second.append(send(mine.at[pl.ds(dest * share, share)], far.at[k], s2.at[k], r2.at[k], at(T * a, T * b)))
    for c in second:
        c.start()
    total = mine[pl.ds(f_me * share, share)]
    for c in second:
        c.wait_recv()
    for k in range(1, nfar):
        total = total + far[k]
    full[pl.ds(f_me * share, share), zl, yl] = total

    third = []
    for a, b in fars:
        k = a * nyh + b
        shard = full.at[pl.ds(f_me * share, share), zl, yl]
        third.append(send(shard, shard, s3.at[k], r3.at[k], at(T * a, T * b)))
    for c in third:
        c.start()
    for c in third:
        c.wait_recv()

    half = blocks_step // 2

    def near(step, turn):
        base = step * blocks_step
        sends, recvs = [], []
        s, r = (s4, r4) if turn == 0 else (s5, r5)
        for i, (dz, dy) in enumerate(NEAR):
            along_z = dy == 0
            lo = base + (0 if along_z == (turn == 0) else half)
            n = half
            if (dz, dy) in ((2, 0), (0, 2)):
                n = half // 2
            if (dz, dy) in ((-2, 0), (0, -2)):
                lo, n = lo + half // 2, half - half // 2
            if turn == 0:
                ref = full.at[pl.ds(lo, n), zl, yl]
            elif along_z:
                ref = full.at[pl.ds(lo, n), zl]
            else:
                ref = full.at[pl.ds(lo, n), :, yl]
            j = step * len(NEAR) + i
            sends.append(send(ref, ref, s.at[j], r.at[j], at(dz, dy)))
        return sends

    fourth = [near(s, 0) for s in range(steps)]
    fifth = [near(s, 1) for s in range(steps)]
    for cs in fourth:
        for c in cs:
            c.start()
    load.wait()
    for s in range(steps):
        for c in fourth[s]:
            c.wait_recv()
        for c in fifth[s]:
            c.start()

    rows = out.shape[0]
    edge = head.shape[1]
    tall = 2 * edge
    has_below = group < groups - 1
    eye = (
        lax.broadcasted_iota(jnp.int32, (edge, edge), 0) == lax.broadcasted_iota(jnp.int32, (edge, edge), 1)
    ).astype(F32)
    halo = []

    def block(b):
        basis = full[b, :, :, 0:vr].reshape(tall, edge)
        factor = full[b, :, :, vr : vr + tr].reshape(edge, edge)
        return split(basis.T), split(factor), split(basis)

    def apply(ops, x):
        w = mul(ops[0], split(x))
        return mul(ops[2], split(mul(ops[1], split(w))))

    for s in range(steps):
        up = send(head.at[s], beneath.at[s], sh.at[2 * s], rh.at[2 * s], row(-1))
        dn = send(down.at[s], delta.at[s], sh.at[2 * s + 1], rh.at[2 * s + 1], row(1))
        halo += [up, dn]
        head[s] = out[0:edge]
        up.start()
        for c in fifth[s]:
            c.wait_recv()
        ident[0:edge] = eye
        ident[edge:] = jnp.zeros((ident.shape[0] - edge, edge), F32)
        for j in range(inner):
            ops = block(s * blocks_step + j)
            o = offs[0, s, j]
            oe = jnp.minimum(o, REACH)
            x = jnp.concatenate([out[pl.ds(o, tall)], ident[pl.ds(oe, tall)]], 1)
            d = apply(ops, x)
            shift_x[rows - tall : rows] = d[:, :edge]
            shift_e[REACH : REACH + tall] = d[:, edge:]
            for i in range(rows // tall):
                out[i * tall : (i + 1) * tall] -= shift_x[pl.ds(rows - tall - o + i * tall, tall)]
            for i in range(REACH // edge):
                ident[i * edge : (i + 1) * edge] -= shift_e[pl.ds(REACH - oe + i * edge, edge)]
        ops = block(s * blocks_step + inner)
        up.wait_recv()
        x = jnp.concatenate([out[rows - edge :], beneath[s]], 0)
        d = jnp.where(has_below, apply(ops, x), 0.0)
        down[s] = d[edge:]
        dn.start()
        out[rows - edge :] -= d[:edge]
        carry = split(ident[0:REACH])
        dn.wait_recv()
        out[0:REACH] -= mul(carry, split(delta[s]))

    for c in first + second + third + halo:
        c.wait_send()
    for cs in fourth + fifth:
        for c in cs:
            c.wait_send()


def solution(mesh):
    groups = mesh.shape["row"]
    nz = mesh.shape["col"] // NY

    def per_device(vectors, reflectors, wy_factors, block_slots, offsets):
        steps, inner = offsets.shape[1:]
        blocks = steps * (inner + 1)
        rows, width = vectors.shape
        hold, tall, edge = reflectors.shape[1:]
        vr, tr = tall // PIECES, edge // PIECES
        nfar = (nz // T) * (NY // T)
        share = blocks // nfar
        dma = pltpu.SemaphoreType.DMA
        vmem = pltpu.VMEM
        return pl.pallas_call(
            functools.partial(kernel, nz, groups, steps, inner),
            out_shape=jax.ShapeDtypeStruct((rows, width), F32),
            in_specs=[pl.BlockSpec(memory_space=pltpu.SMEM)] * 2 + [pl.BlockSpec(memory_space=pl.ANY)] * 3,
            out_specs=pl.BlockSpec(memory_space=pltpu.VMEM),
            scratch_shapes=[
                vmem((PIECES, hold, vr, edge), F32),
                vmem((PIECES, hold, tr, edge), F32),
                vmem((blocks, vr + tr, edge), F32),
                vmem((nfar, share, vr + tr, edge), F32),
                vmem((blocks, T, T, vr + tr, edge), F32),
                vmem((REACH + tall, width), F32),
                vmem((2 * rows - tall, width), F32),
                vmem((2 * REACH, width), F32),
                vmem((steps, edge, width), F32),
                vmem((steps, edge, width), F32),
                vmem((steps, edge, width), F32),
                vmem((steps, edge, width), F32),
                dma((3,)),
                dma((2 * PIECES,)), dma((2 * PIECES,)),
                dma((nfar,)), dma((nfar,)),
                dma((nfar,)), dma((nfar,)),
                dma((steps * len(NEAR),)), dma((steps * len(NEAR),)),
                dma((steps * len(NEAR),)), dma((steps * len(NEAR),)),
                dma((2 * steps,)), dma((2 * steps,)),
            ],
            compiler_params=pltpu.CompilerParams(
                collective_id=0, has_side_effects=True, vmem_limit_bytes=40 * 1024 * 1024
            ),
        )(block_slots, offsets, vectors, reflectors, wy_factors)

    in_specs = (
        P("row", "col"),
        P("row", "col", None, None),
        P("row", "col", None, None),
        P("row", None, None),
        P("row", None, None),
    )
    return jax.shard_map(per_device, mesh=mesh, in_specs=in_specs, out_specs=P("row", "col"), check_vma=False)
```

```python
import functools

import jax
import jax.numpy as jnp
from jax import lax
from jax.experimental import pallas as pl
from jax.experimental.pallas import tpu as pltpu
from jax.sharding import PartitionSpec as P

MESH = pl.DeviceIdType.MESH
F32 = jnp.float32
BF16 = jnp.bfloat16
NY = 8
T = 4
PIECES = T * T
REACH = 896
FAR_REACH = 1664

TILE = [(dz, dy) for dz in (-1, 0, 1, 2) for dy in (-1, 0, 1, 2)]
NEAR = [(1, 0), (-1, 0), (2, 0), (-2, 0), (0, 1), (0, -1), (0, 2), (0, -2)]


def split(x):
    high = x.astype(BF16)
    return high, (x - high.astype(F32)).astype(BF16)


def mul(a, b):
    (ah, al), (bh, bl) = a, b
    dot = functools.partial(jnp.dot, preferred_element_type=F32)
    return dot(ah, bh) + (dot(ah, bl) + dot(al, bh))


def kernel(
    nz, groups, steps, inner,
    slots, offs, vec, refl, wy, out,
    got_v, got_t, mine, far, full, ident, pending, shift_x, shift_e, shift_p, head, beneath, down, delta,
    load_sem, relay, s1, r1, s2, r2, s3, r3, s4, r4, s5, r5, sh, rh,
):
    blocks_step = inner + 1
    blocks = steps * blocks_step
    nzh, nyh = nz // T, NY // T
    nfar = nzh * nyh
    group = lax.axis_index("row")
    col = lax.axis_index("col")
    z, y = col // NY, col % NY
    zl, yl, zh, yh = z % T, y % T, z // T, y // T
    f_me = zh * nyh + yh
    p_me = zl * T + yl

    def at(dz, dy):
        return {"col": ((z + dz + nz) % nz) * NY + (y + dy + NY) % NY}

    def row(d):
        return {"row": (group + d + groups) % groups}

    def send(src, dst, ssem, rsem, dev):
        return pltpu.make_async_remote_copy(
            src_ref=src, dst_ref=dst, send_sem=ssem, recv_sem=rsem, device_id=dev, device_id_type=MESH
        )

    fars = [(a, b) for a in range(nzh) for b in range(nyh) if (a, b) != (0, 0)]
    fars = sorted(fars, key=lambda ab: (ab[0] == nzh // 2 and ab[1] > 0))

    load = pltpu.make_async_copy(vec, out, load_sem.at[0])
    load.start()

    greet = {(-dz, -dy) for dz, dy in TILE} | set(NEAR) | {(T, 0), (-T, 0), (0, T)}
    greet = sorted({(dz % nz, dy % NY) for dz, dy in greet} - {(0, 0)})
    barrier = pltpu.get_barrier_semaphore()
    for dz, dy in greet:
        pl.semaphore_signal(barrier, inc=1, device_id=at(dz, dy), device_id_type=MESH)
    for d in (1, -1):
        pl.semaphore_signal(barrier, inc=1, device_id=row(d), device_id_type=MESH)
    pl.semaphore_wait(barrier, len(greet) + 2)
    for i, (dz, dy) in enumerate([(T, 0), (-T, 0), (0, T)]):
        pl.semaphore_signal(relay.at[i], inc=1, device_id=at(dz, dy), device_id_type=MESH)

    first, own = [], []
    vr = got_v.shape[2]
    tr = got_t.shape[2]
    for k, (dz, dy) in enumerate(TILE):
        p = ((z + dz + nz) % T) * T + (y + dy + NY) % T
        src_v = refl.at[0, :, pl.ds(pl.multiple_of(p * vr, vr), vr)]
        src_t = wy.at[0, :, pl.ds(pl.multiple_of(p * tr, tr), tr)]
        if (dz, dy) == (0, 0):
            own = [
                pltpu.make_async_copy(src_v, got_v.at[k], load_sem.at[1]),
                pltpu.make_async_copy(src_t, got_t.at[k], load_sem.at[2]),
            ]
        else:
            first += [
                send(src_v, got_v.at[k], s1.at[k], r1.at[k], at(dz, dy)),
                send(src_t, got_t.at[k], s1.at[k + PIECES], r1.at[k + PIECES], at(dz, dy)),
            ]
    for c in first + own:
        c.start()

    shift_x[...] = jnp.zeros_like(shift_x)
    shift_e[...] = jnp.zeros_like(shift_e)
    shift_p[...] = jnp.zeros_like(shift_p)
    for c in own:
        c.wait()
    for i in range(3):
        pl.semaphore_wait(relay.at[i], 1)
    pl.semaphore_signal(relay.at[3], inc=1, device_id=at(0, T), device_id_type=MESH)
    for c in first:
        c.wait_recv()

    lots = blocks // nfar
    second, third = [], []
    for lot in range(lots):
        for b in range(lot * nfar, (lot + 1) * nfar):
            slot = slots[0, b // blocks_step, b % blocks_step]
            root = slot // 2
            az = (z - root // NY + nz + 1) % nz
            ay = (y - root % NY + NY + 1) % NY
            here = jnp.logical_and(az < T, ay < T)
            k = jnp.minimum(az, T - 1) * T + jnp.minimum(ay, T - 1)
            half = slot % 2
            mine[b, 0:vr] = jnp.where(here, got_v[k, half], 0.0)
            mine[b, vr : vr + tr] = jnp.where(here, got_t[k, half], 0.0)
        sends = []
        for a, b in fars:
            k = a * nyh + b
            dest = lot * nfar + ((zh + a) % nzh) * nyh + (yh + b) % nyh
            j = lot * nfar + k
            sends.append(send(mine.at[dest], far.at[lot, k], s2.at[j], r2.at[j], at(T * a, T * b)))
        for (a, b), c in zip(fars, sends):
            if lot == 0 and (a, b) == fars[-1]:
                pl.semaphore_wait(relay.at[3], 1)
            c.start()
        second.append(sends)

    for lot in range(lots):
        me = lot * nfar + f_me
        total = mine[me]
        for c in second[lot]:
            c.wait_recv()
        for k in range(1, nfar):
            total = total + far[lot, k]
        full[me, zl, yl] = total
        sends = []
        for a, b in fars:
            j = lot * nfar + a * nyh + b
            shard = full.at[me, zl, yl]
            sends.append(send(shard, shard, s3.at[j], r3.at[j], at(T * a, T * b)))
        for c in sends:
            c.start()
        third.append(sends)

    half = blocks_step // 2

    def near(step, turn):
        base = step * blocks_step
        sends, recvs = [], []
        s, r = (s4, r4) if turn == 0 else (s5, r5)
        for i, (dz, dy) in enumerate(NEAR):
            along_z = dy == 0
            lo = base + (0 if along_z == (turn == 0) else half)
            n = half
            if (dz, dy) in ((2, 0), (0, 2)):
                n = half // 2
            if (dz, dy) in ((-2, 0), (0, -2)):
                lo, n = lo + half // 2, half - half // 2
            if turn == 0:
                ref = full.at[pl.ds(lo, n), zl, yl]
            elif along_z:
                ref = full.at[pl.ds(lo, n), zl]
            else:
                ref = full.at[pl.ds(lo, n), :, yl]
            j = step * len(NEAR) + i
            sends.append(send(ref, ref, s.at[j], r.at[j], at(dz, dy)))
        return sends

    fourth = [near(s, 0) for s in range(steps)]
    fifth = [near(s, 1) for s in range(steps)]
    for lot in range(lots):
        for c in third[lot]:
            c.wait_recv()
        for s in range(lot * steps // lots, (lot + 1) * steps // lots):
            for c in fourth[s]:
                c.start()
    load.wait()
    for s in range(steps):
        for c in fourth[s]:
            c.wait_recv()
        for c in fifth[s]:
            c.start()

    rows = out.shape[0]
    edge = head.shape[2]
    tall = 2 * edge
    has_below = group < groups - 1
    eye = (
        lax.broadcasted_iota(jnp.int32, (edge, edge), 0) == lax.broadcasted_iota(jnp.int32, (edge, edge), 1)
    ).astype(F32)
    halo = []

    def block(b):
        basis = full[b, :, :, 0:vr].reshape(tall, edge)
        factor = full[b, :, :, vr : vr + tr].reshape(edge, edge)
        return split(basis.T), split(factor), split(basis)

    def apply(ops, x):
        w = mul(ops[0], split(x))
        return mul(ops[2], split(mul(ops[1], split(w))))

    def place(target, shift, d, o, reach, chunk):
        start = jnp.minimum(o, reach)
        shift[reach : reach + tall] = d
        for i in range(0, reach + (tall if reach + tall == rows else 0), chunk):
            target[i : i + chunk] -= shift[pl.ds(reach - start + i, chunk)]

    head[0, 0] = out[0:edge]
    up = send(head.at[0, 0], beneath.at[0, 0], sh.at[0], rh.at[0], row(-1))
    up.start()
    ups, dns = [up], []
    for c in first:
        c.wait_send()
    for cs in second + third:
        for c in cs:
            c.wait_send()
    for s in range(steps):
        for c in fourth[s] + (fifth[s - 1] if s > 0 else []):
            c.wait_send()
        for c in fifth[s]:
            c.wait_recv()
        ident[0:edge] = eye
        ident[edge:] = jnp.zeros((ident.shape[0] - edge, edge), F32)
        for j in range(inner):
            ops = block(s * blocks_step + j)
            o = offs[0, s, j]
            x = [out[pl.ds(o, tall)], ident[pl.ds(jnp.minimum(o, REACH), tall)]]
            if s > 0:
                x.append(pending[pl.ds(jnp.minimum(o, FAR_REACH), tall)])
            d = apply(ops, jnp.concatenate(x, 1))
            place(out, shift_x, d[:, :edge], o, rows - tall, tall)
            place(ident, shift_e, d[:, edge : 2 * edge], o, REACH, edge)
            if s > 0:
                place(pending, shift_p, d[:, 2 * edge :], o, FAR_REACH, edge)
        ups[s].wait_recv()
        under = beneath[s, 0]
        if s > 0:
            under = under - mul(split(beneath[s, 1]), split(down[s - 1]))
        ops = block(s * blocks_step + inner)
        d = jnp.where(has_below, apply(ops, jnp.concatenate([out[rows - edge :], under], 0)), 0.0)
        down[s] = d[edge:]
        dn = send(down.at[s], delta.at[s], sh.at[steps + s], rh.at[steps + s], row(1))
        dn.start()
        dns.append(dn)
        out[rows - edge :] -= d[:edge]
        if s > 0:
            dns[s - 1].wait_recv()
            out[0:FAR_REACH] -= mul(split(pending[0:FAR_REACH]), split(delta[s - 1]))
        if s < steps - 1:
            head[s + 1, 0] = out[0:edge]
            head[s + 1, 1] = ident[0:edge]
            up = send(head.at[s + 1], beneath.at[s + 1], sh.at[s + 1], rh.at[s + 1], row(-1))
            up.start()
            ups.append(up)
            pending[0:REACH] = ident[0:REACH]
            pending[REACH:] = jnp.zeros((pending.shape[0] - REACH, edge), F32)
    dns[steps - 1].wait_recv()
    out[0:REACH] -= mul(split(ident[0:REACH]), split(delta[steps - 1]))
    halo = ups + dns

    for c in fifth[steps - 1] + halo:
        c.wait_send()


def solution(mesh):
    groups = mesh.shape["row"]
    nz = mesh.shape["col"] // NY

    def per_device(vectors, reflectors, wy_factors, block_slots, offsets):
        steps, inner = offsets.shape[1:]
        blocks = steps * (inner + 1)
        rows, width = vectors.shape
        hold, tall, edge = reflectors.shape[1:]
        vr, tr = tall // PIECES, edge // PIECES
        nfar = (nz // T) * (NY // T)
        dma = pltpu.SemaphoreType.DMA
        vmem = pltpu.VMEM
        return pl.pallas_call(
            functools.partial(kernel, nz, groups, steps, inner),
            out_shape=jax.ShapeDtypeStruct((rows, width), F32),
            in_specs=[pl.BlockSpec(memory_space=pltpu.SMEM)] * 2 + [pl.BlockSpec(memory_space=pl.ANY)] * 3,
            out_specs=pl.BlockSpec(memory_space=pltpu.VMEM),
            scratch_shapes=[
                vmem((PIECES, hold, vr, edge), F32),
                vmem((PIECES, hold, tr, edge), F32),
                vmem((blocks, vr + tr, edge), F32),
                vmem((blocks // nfar, nfar, vr + tr, edge), F32),
                vmem((blocks, T, T, vr + tr, edge), F32),
                vmem((REACH + tall, width), F32),
                vmem((FAR_REACH + tall, width), F32),
                vmem((2 * rows - tall, width), F32),
                vmem((2 * REACH, width), F32),
                vmem((2 * FAR_REACH, width), F32),
                vmem((steps, 2, edge, width), F32),
                vmem((steps, 2, edge, width), F32),
                vmem((steps, edge, width), F32),
                vmem((steps, edge, width), F32),
                dma((3,)),
                pltpu.SemaphoreType.REGULAR((4,)),
                dma((2 * PIECES,)), dma((2 * PIECES,)),
                dma((blocks,)), dma((blocks,)),
                dma((blocks,)), dma((blocks,)),
                dma((steps * len(NEAR),)), dma((steps * len(NEAR),)),
                dma((steps * len(NEAR),)), dma((steps * len(NEAR),)),
                dma((2 * steps,)), dma((2 * steps,)),
            ],
            compiler_params=pltpu.CompilerParams(
                collective_id=0, has_side_effects=True, vmem_limit_bytes=40 * 1024 * 1024
            ),
        )(block_slots, offsets, vectors, reflectors, wy_factors)

    in_specs = (
        P("row", "col"),
        P("row", "col", None, None),
        P("row", "col", None, None),
        P("row", None, None),
        P("row", None, None),
    )
    return jax.shard_map(per_device, mesh=mesh, in_specs=in_specs, out_specs=P("row", "col"), check_vma=False)
```

```python
import functools

import jax
import jax.numpy as jnp
from jax import lax
from jax.experimental import pallas as pl
from jax.experimental.pallas import tpu as pltpu
from jax.sharding import PartitionSpec as P

MESH = pl.DeviceIdType.MESH
F32 = jnp.float32
BF16 = jnp.bfloat16
NY = 8
T = 4
PIECES = T * T
REACH = 896
FAR_REACH = 1664

TILE = [(dz, dy) for dz in (-1, 0, 1, 2) for dy in (-1, 0, 1, 2)]
NEAR = [(1, 0), (-1, 0), (2, 0), (-2, 0), (0, 1), (0, -1), (0, 2), (0, -2)]


def split(x):
    high = x.astype(BF16)
    return high, (x - high.astype(F32)).astype(BF16)


def mul(a, b):
    (ah, al), (bh, bl) = a, b
    dot = functools.partial(jnp.dot, preferred_element_type=F32)
    return dot(ah, bh) + (dot(ah, bl) + dot(al, bh))


def iotas(shape):
    return lax.broadcasted_iota(jnp.int32, shape, 0), lax.broadcasted_iota(jnp.int32, shape, 1)


def pack(basis, factor):
    edge = factor.shape[0]
    mid = edge // 2
    r, c = iotas((edge, edge))
    diag = jnp.where(r == c, factor, 0.0)
    along = jnp.sqrt(jnp.sum(diag, 0, keepdims=True))
    down = jnp.sqrt(jnp.sum(diag, 1, keepdims=True))
    unit = factor / (along * down)
    turned = jnp.concatenate([unit[mid:], jnp.zeros((mid, edge), F32)], 0).T[mid:]
    r, c = iotas((mid, edge))
    return basis * along, jnp.where(jnp.logical_and(c < mid, r > c), turned, unit[:mid])


def unpack(folded):
    mid, edge = folded.shape
    r, c = iotas((mid, edge))
    turned = jnp.concatenate([jnp.zeros((mid, edge), F32), folded], 0).T[:mid]
    top = jnp.where(c > r, folded, jnp.where(c == r, 1.0, 0.0))
    low = jnp.where(c > r + mid, turned, jnp.where(c == r + mid, 1.0, 0.0))
    return jnp.concatenate([top, low], 0)


def kernel(
    nz, groups, steps, inner,
    slots, offs, vec, refl, wy, out,
    base, fold, got_v, got_t, mine, far, far_t, full, ident, pending, shift_x, shift_e, shift_p, head, beneath, down, delta,
    load_sem, relay, s1, r1, s2, r2, s3, r3, st, rt, s4, r4, s5, r5, sh, rh,
):
    blocks_step = inner + 1
    blocks = steps * blocks_step
    nzh, nyh = nz // T, NY // T
    nfar = nzh * nyh
    group = lax.axis_index("row")
    col = lax.axis_index("col")
    z, y = col // NY, col % NY
    zl, yl, zh, yh = z % T, y % T, z // T, y // T
    f_me = zh * nyh + yh
    p_me = zl * T + yl

    def at(dz, dy):
        return {"col": ((z + dz + nz) % nz) * NY + (y + dy + NY) % NY}

    def row(d):
        return {"row": (group + d + groups) % groups}

    def send(src, dst, ssem, rsem, dev):
        return pltpu.make_async_remote_copy(
            src_ref=src, dst_ref=dst, send_sem=ssem, recv_sem=rsem, device_id=dev, device_id_type=MESH
        )

    fars = [(a, b) for a in range(nzh) for b in range(nyh) if (a, b) != (0, 0)]
    fars = sorted(fars, key=lambda ab: (ab[0] == nzh // 2 and ab[1] > 0))

    load = pltpu.make_async_copy(vec, out, load_sem.at[0])
    load.start()

    greet = {(-dz, -dy) for dz, dy in TILE} | set(NEAR) | {(T, 0), (-T, 0), (0, T)}
    greet = sorted({(dz % nz, dy % NY) for dz, dy in greet} - {(0, 0)})
    barrier = pltpu.get_barrier_semaphore()
    for dz, dy in greet:
        pl.semaphore_signal(barrier, inc=1, device_id=at(dz, dy), device_id_type=MESH)
    for d in (1, -1):
        pl.semaphore_signal(barrier, inc=1, device_id=row(d), device_id_type=MESH)
    copies = [
        pltpu.make_async_copy(refl.at[0], base, load_sem.at[1]),
        pltpu.make_async_copy(wy.at[0], fold, load_sem.at[2]),
    ]
    for c in copies:
        c.start()
    for c in copies:
        c.wait()
    mid = fold.shape[1] // 2
    for h in range(base.shape[0]):
        base[h], fold[h, 0:mid] = pack(base[h], fold[h])
    pl.semaphore_wait(barrier, len(greet) + 2)
    for i, (dz, dy) in enumerate([(T, 0), (-T, 0), (0, T)]):
        pl.semaphore_signal(relay.at[i], inc=1, device_id=at(dz, dy), device_id_type=MESH)

    first, own = [], []
    vr = got_v.shape[2]
    tr = got_t.shape[2]
    for k, (dz, dy) in enumerate(TILE):
        p = ((z + dz + nz) % T) * T + (y + dy + NY) % T
        src_v = base.at[:, pl.ds(pl.multiple_of(p * vr, vr), vr)]
        src_t = fold.at[:, pl.ds(pl.multiple_of(p % (PIECES // 2) * tr, tr), tr)]
        if (dz, dy) == (0, 0):
            own = [
                pltpu.make_async_copy(src_v, got_v.at[k], load_sem.at[3]),
                pltpu.make_async_copy(src_t, got_t.at[k], load_sem.at[4]),
            ]
        else:
            first += [
                send(src_v, got_v.at[k], s1.at[k], r1.at[k], at(dz, dy)),
                send(src_t, got_t.at[k], s1.at[k + PIECES], r1.at[k + PIECES], at(dz, dy)),
            ]
    for c in first + own:
        c.start()

    ident[...] = jnp.zeros_like(ident)
    shift_x[...] = jnp.zeros_like(shift_x)
    shift_e[...] = jnp.zeros_like(shift_e)
    shift_p[...] = jnp.zeros_like(shift_p)
    for c in own:
        c.wait()
    for i in range(3):
        pl.semaphore_wait(relay.at[i], 1)
    pl.semaphore_signal(relay.at[3], inc=1, device_id=at(0, T), device_id_type=MESH)
    for c in first:
        c.wait_recv()

    lots = steps
    second, third = [], []
    rest = 2 * vr
    unit = blocks_step * vr // nfar
    units = rest // unit

    def place_of(lot, f):
        return lot * blocks_step // 2 + f // units, pl.ds(pl.multiple_of(f % units * unit, unit), unit)

    def where_is(slot):
        root = slot // 2
        az = (z - root // NY + nz + 1) % nz
        ay = (y - root % NY + NY + 1) % NY
        here = jnp.logical_and(az < T, ay < T)
        return here, jnp.minimum(az, T - 1) * T + jnp.minimum(ay, T - 1), slot % 2

    for lot in range(lots):
        sends = []
        for b in range(lot * blocks_step, (lot + 1) * blocks_step):
            here, k, half = where_is(slots[0, b // blocks_step, b % blocks_step])
            mine[b // 2, (b % 2) * vr : (b % 2 + 1) * vr] = jnp.where(here, got_v[k, half], 0.0)
        if lot == 0:
            for q in range(blocks // 2):
                one = slots[0, 2 * q // blocks_step, 2 * q % blocks_step]
                two = slots[0, (2 * q + 1) // blocks_step, (2 * q + 1) % blocks_step]
                here, k, half = where_is(jnp.where(p_me < PIECES // 2, one, two))
                mine[q, rest : rest + tr] = jnp.where(here, got_t[k, half], 0.0)
        for a, b in fars:
            k = a * nyh + b
            dest = ((zh + a) % nzh) * nyh + (yh + b) % nyh
            q, part = place_of(lot, dest)
            j = lot * nfar + k
            dev = at(T * a, T * b)
            sends.append(send(mine.at[q, part], far.at[lot, k], s2.at[j], r2.at[j], dev))
            if lot == 0:
                src = mine.at[dest, rest : rest + tr]
                sends.append(send(src, far_t.at[k], st.at[k], rt.at[k], dev))
        for i, c in enumerate(sends):
            if lot == 0 and i == 2 * (nfar - 2):
                pl.semaphore_wait(relay.at[3], 1)
            c.start()
        second.append(sends)

    for lot in range(lots):
        me, part = place_of(lot, f_me)
        total = mine[me, part]
        for c in second[lot]:
            c.wait_recv()
        for k in range(1, nfar):
            total = total + far[lot, k]
        full[me, zl, yl, part] = total
        shards = [full.at[me, zl, yl, part]]
        if lot == 0:
            total = mine[f_me, rest : rest + tr]
            for k in range(1, nfar):
                total = total + far_t[k]
            full[f_me, zl, yl, rest : rest + tr] = total
            shards.append(full.at[f_me, zl, yl, rest : rest + tr])
        sends = []
        for a, b in fars:
            k = a * nyh + b
            j = lot * nfar + k
            for i, shard in enumerate(shards):
                ssem, rsem = (s3.at[j], r3.at[j]) if i == 0 else (st.at[nfar + k], rt.at[nfar + k])
                sends.append(send(shard, shard, ssem, rsem, at(T * a, T * b)))
        for c in sends:
            c.start()
        third.append(sends)

    pairs = blocks_step // 2

    def near(step, turn):
        sends = []
        s, r = (s4, r4) if turn == 0 else (s5, r5)
        for i, (dz, dy) in enumerate(NEAR):
            along_z = dy == 0
            lo, n = step * pairs + (0 if along_z == (turn == 0) else pairs // 2), pairs // 2
            rows = slice(0, rest + tr)
            if abs(dz + dy) == 2:
                rows = slice(0, vr) if (dz + dy > 0) == (step % 2 == 0) else slice(vr, rest + tr)
            if turn == 0:
                ref = full.at[pl.ds(lo, n), zl, yl, rows]
            elif along_z:
                ref = full.at[pl.ds(lo, n), zl, :, rows]
            else:
                ref = full.at[pl.ds(lo, n), :, yl, rows]
            j = step * len(NEAR) + i
            sends.append(send(ref, ref, s.at[j], r.at[j], at(dz, dy)))
        return sends

    fourth = [near(s, 0) for s in range(steps)]
    fifth = [near(s, 1) for s in range(steps)]
    for lot in range(lots):
        for c in third[lot]:
            c.wait_recv()
        for s in range(lot * steps // lots, (lot + 1) * steps // lots):
            for c in fourth[s]:
                c.start()
    load.wait()
    for s in range(steps):
        for c in fourth[s]:
            c.wait_recv()
        for c in fifth[s]:
            c.start()

    rows = out.shape[0]
    edge = head.shape[2]
    tall = 2 * edge
    has_below = group < groups - 1
    eye = (
        lax.broadcasted_iota(jnp.int32, (edge, edge), 0) == lax.broadcasted_iota(jnp.int32, (edge, edge), 1)
    ).astype(F32)
    halo = []

    def block(b):
        h = b % 2
        basis = full[b // 2, :, :, h * vr : (h + 1) * vr].reshape(tall, edge)
        factor = unpack(full[b // 2, h * T // 2 : (h + 1) * T // 2, :, rest : rest + tr].reshape(edge // 2, edge))
        return split(basis.T), split(factor), split(basis)

    def apply(ops, x):
        w = mul(ops[0], split(x))
        return mul(ops[2], split(mul(ops[1], split(w))))

    ident[0:edge] = eye

    def window(target, shifts, starts, start, reach, count):
        x = target[pl.ds(start, count)]
        for shift, o in zip(shifts, starts):
            x = x - shift[pl.ds(reach - o + start, count)]
        return x

    head[0, 0] = out[0:edge]
    up = send(head.at[0, 0], beneath.at[0, 0], sh.at[0], rh.at[0], row(-1))
    up.start()
    ups, dns = [up], []
    for c in first:
        c.wait_send()
    for cs in second + third:
        for c in cs:
            c.wait_send()
    for s in range(steps):
        for c in fourth[s] + (fifth[s - 1] if s > 0 else []):
            c.wait_send()
        for c in fifth[s]:
            c.wait_recv()
        at_x, at_e, at_p, parts = [], [], [], []
        for j in range(inner):
            ops = block(s * blocks_step + j)
            o = offs[0, s, j]
            oe, op = jnp.minimum(o, REACH), jnp.minimum(o, FAR_REACH)
            x = [
                window(out, [shift_x.at[i] for i in range(j)], at_x, o, rows - tall, tall),
                window(ident, [shift_e.at[i] for i in range(j)], at_e, oe, REACH, tall),
            ]
            if s > 0:
                x.append(window(pending, [shift_p.at[i] for i in range(j)], at_p, op, FAR_REACH, tall))
            d = apply(ops, jnp.concatenate(x, 1))
            shift_x[j, rows - tall : rows] = d[:, :edge]
            shift_e[j, REACH : REACH + tall] = d[:, edge : 2 * edge]
            if s > 0:
                shift_p[j, FAR_REACH : FAR_REACH + tall] = d[:, 2 * edge :]
            at_x, at_e, at_p = at_x + [o], at_e + [oe], at_p + [op]
        all_x, all_e, all_p = ([f.at[i] for i in range(inner)] for f in (shift_x, shift_e, shift_p))
        ups[s].wait_recv()
        under = beneath[s, 0]
        if s > 0:
            under = under - mul(split(beneath[s, 1]), split(down[s - 1]))
        ops = block(s * blocks_step + inner)
        tail = window(out, all_x, at_x, rows - edge, rows - tall, edge)
        d = jnp.where(has_below, apply(ops, jnp.concatenate([tail, under], 0)), 0.0)
        down[s] = d[edge:]
        dn = send(down.at[s], delta.at[s], sh.at[steps + s], rh.at[steps + s], row(1))
        dn.start()
        dns.append(dn)
        for i in range(0, rows - edge, edge):
            out[i : i + edge] = window(out, all_x, at_x, i, rows - tall, edge)
        out[rows - edge :] = tail - d[:edge]
        if s > 0:
            dns[s - 1].wait_recv()
            coming = split(delta[s - 1])
            carry = window(pending, all_p, at_p, 0, FAR_REACH, FAR_REACH)
            out[0:FAR_REACH] -= mul(split(carry), coming)
        for i in range(0, REACH, edge):
            pending[i : i + edge] = window(ident, all_e, at_e, i, REACH, edge)
        if s == 0:
            pending[REACH:] = jnp.zeros((pending.shape[0] - REACH, edge), F32)
        if s < steps - 1:
            head[s + 1, 0] = out[0:edge]
            head[s + 1, 1] = pending[0:edge]
            up = send(head.at[s + 1], beneath.at[s + 1], sh.at[s + 1], rh.at[s + 1], row(-1))
            up.start()
            ups.append(up)
    dns[steps - 1].wait_recv()
    out[0:REACH] -= mul(split(pending[0:REACH]), split(delta[steps - 1]))
    halo = ups + dns

    for c in fifth[steps - 1] + halo:
        c.wait_send()


def solution(mesh):
    groups = mesh.shape["row"]
    nz = mesh.shape["col"] // NY

    def per_device(vectors, reflectors, wy_factors, block_slots, offsets):
        steps, inner = offsets.shape[1:]
        blocks = steps * (inner + 1)
        rows, width = vectors.shape
        hold, tall, edge = reflectors.shape[1:]
        vr, tr = tall // PIECES, edge // PIECES
        nfar = (nz // T) * (NY // T)
        dma = pltpu.SemaphoreType.DMA
        vmem = pltpu.VMEM
        return pl.pallas_call(
            functools.partial(kernel, nz, groups, steps, inner),
            out_shape=jax.ShapeDtypeStruct((rows, width), F32),
            in_specs=[pl.BlockSpec(memory_space=pltpu.SMEM)] * 2 + [pl.BlockSpec(memory_space=pl.ANY)] * 3,
            out_specs=pl.BlockSpec(memory_space=pltpu.VMEM),
            scratch_shapes=[
                vmem((hold, tall, edge), F32),
                vmem((hold, edge, edge), F32),
                vmem((PIECES, hold, vr, edge), F32),
                vmem((PIECES, hold, tr, edge), F32),
                vmem((blocks // 2, 2 * vr + tr, edge), F32),
                vmem((steps, nfar, (inner + 1) * vr // nfar, edge), F32),
                vmem((nfar, tr, edge), F32),
                vmem((blocks // 2, T, T, 2 * vr + tr, edge), F32),
                vmem((REACH + tall, width), F32),
                vmem((FAR_REACH + tall, width), F32),
                vmem((inner, 2 * rows - tall, width), F32),
                vmem((inner, 2 * REACH + tall, width), F32),
                vmem((inner, 2 * FAR_REACH + tall, width), F32),
                vmem((steps, 2, edge, width), F32),
                vmem((steps, 2, edge, width), F32),
                vmem((steps, edge, width), F32),
                vmem((steps, edge, width), F32),
                dma((5,)),
                pltpu.SemaphoreType.REGULAR((4,)),
                dma((2 * PIECES,)), dma((2 * PIECES,)),
                dma((steps * nfar,)), dma((steps * nfar,)),
                dma((steps * nfar,)), dma((steps * nfar,)),
                dma((2 * nfar,)), dma((2 * nfar,)),
                dma((steps * len(NEAR),)), dma((steps * len(NEAR),)),
                dma((steps * len(NEAR),)), dma((steps * len(NEAR),)),
                dma((2 * steps,)), dma((2 * steps,)),
            ],
            compiler_params=pltpu.CompilerParams(
                collective_id=0, has_side_effects=True, vmem_limit_bytes=40 * 1024 * 1024
            ),
        )(block_slots, offsets, vectors, reflectors, wy_factors)

    in_specs = (
        P("row", "col"),
        P("row", "col", None, None),
        P("row", "col", None, None),
        P("row", None, None),
        P("row", None, None),
    )
    return jax.shard_map(per_device, mesh=mesh, in_specs=in_specs, out_specs=P("row", "col"), check_vma=False)
```

```python
import functools

import jax
import jax.numpy as jnp
from jax import lax
from jax.experimental import pallas as pl
from jax.experimental.pallas import tpu as pltpu
from jax.sharding import PartitionSpec as P

MESH = pl.DeviceIdType.MESH
F32 = jnp.float32
BF16 = jnp.bfloat16
NY = 8
T = 4
PIECES = T * T
REACH = 896
FAR_REACH = 1664

TILE = [(dz, dy) for dz in (-1, 0, 1, 2) for dy in (-1, 0, 1, 2)]
NEAR = [(1, 0), (-1, 0), (2, 0), (-2, 0), (0, 1), (0, -1), (0, 2), (0, -2)]


def split(x):
    high = x.astype(BF16)
    return high, (x - high.astype(F32)).astype(BF16)


def mul(a, b):
    (ah, al), (bh, bl) = a, b
    dot = functools.partial(jnp.dot, preferred_element_type=F32)
    return dot(ah, bh) + (dot(ah, bl) + dot(al, bh))


def iotas(shape):
    return lax.broadcasted_iota(jnp.int32, shape, 0), lax.broadcasted_iota(jnp.int32, shape, 1)


def pack(basis, factor):
    edge = factor.shape[0]
    mid = edge // 2
    r, c = iotas((edge, edge))
    diag = jnp.where(r == c, factor, 0.0)
    along = jnp.sqrt(jnp.sum(diag, 0, keepdims=True))
    down = jnp.sqrt(jnp.sum(diag, 1, keepdims=True))
    unit = factor / (along * down)
    turned = jnp.concatenate([unit[mid:], jnp.zeros((mid, edge), F32)], 0).T[mid:]
    r, c = iotas((mid, edge))
    return basis * along, jnp.where(jnp.logical_and(c < mid, r > c), turned, unit[:mid])


def unpack(folded):
    mid, edge = folded.shape
    r, c = iotas((mid, edge))
    turned = jnp.concatenate([jnp.zeros((mid, edge), F32), folded], 0).T[:mid]
    top = jnp.where(c > r, folded, jnp.where(c == r, 1.0, 0.0))
    low = jnp.where(c > r + mid, turned, jnp.where(c == r + mid, 1.0, 0.0))
    return jnp.concatenate([top, low], 0)


def kernel(
    nz, groups, steps, inner,
    slots, offs, vec, refl, wy, out,
    base, fold, got_v, got_t, mine, far, far_t, full, ident, pending, shift_x, shift_e, shift_p, head, beneath, down, delta,
    load_sem, relay, s1, r1, s2, r2, s3, r3, st, rt, s4, r4, s5, r5, sh, rh,
):
    blocks_step = inner + 1
    blocks = steps * blocks_step
    nzh, nyh = nz // T, NY // T
    nfar = nzh * nyh
    group = lax.axis_index("row")
    col = lax.axis_index("col")
    z, y = col // NY, col % NY
    zl, yl, zh, yh = z % T, y % T, z // T, y // T
    f_me = zh * nyh + yh
    p_me = zl * T + yl

    def at(dz, dy):
        return {"col": ((z + dz + nz) % nz) * NY + (y + dy + NY) % NY}

    def row(d):
        return {"row": (group + d + groups) % groups}

    def send(src, dst, ssem, rsem, dev):
        return pltpu.make_async_remote_copy(
            src_ref=src, dst_ref=dst, send_sem=ssem, recv_sem=rsem, device_id=dev, device_id_type=MESH
        )

    fars = [(a, b) for a in range(nzh) for b in range(nyh) if (a, b) != (0, 0)]
    fars = sorted(fars, key=lambda ab: (ab[0] == nzh // 2 and ab[1] > 0))

    load = pltpu.make_async_copy(vec, out, load_sem.at[0])
    load.start()

    greet = {(-dz, -dy) for dz, dy in TILE} | set(NEAR) | {(T, 0), (-T, 0), (0, T)}
    greet = sorted({(dz % nz, dy % NY) for dz, dy in greet} - {(0, 0)})
    barrier = pltpu.get_barrier_semaphore()
    for dz, dy in greet:
        pl.semaphore_signal(barrier, inc=1, device_id=at(dz, dy), device_id_type=MESH)
    for d in (1, -1):
        pl.semaphore_signal(barrier, inc=1, device_id=row(d), device_id_type=MESH)
    copies = [
        pltpu.make_async_copy(refl.at[0], base, load_sem.at[1]),
        pltpu.make_async_copy(wy.at[0], fold, load_sem.at[2]),
    ]
    for c in copies:
        c.start()
    for c in copies:
        c.wait()
    mid = fold.shape[1] // 2
    for h in range(base.shape[0]):
        base[h], fold[h, 0:mid] = pack(base[h], fold[h])
    pl.semaphore_wait(barrier, len(greet) + 2)
    for i, (dz, dy) in enumerate([(T, 0), (-T, 0), (0, T)]):
        pl.semaphore_signal(relay.at[i], inc=1, device_id=at(dz, dy), device_id_type=MESH)

    first, own = [], []
    vr = got_v.shape[2]
    tr = got_t.shape[2]
    for k, (dz, dy) in enumerate(TILE):
        p = ((z + dz + nz) % T) * T + (y + dy + NY) % T
        src_v = base.at[:, pl.ds(pl.multiple_of(p * vr, vr), vr)]
        src_t = fold.at[:, pl.ds(pl.multiple_of(p % (PIECES // 2) * tr, tr), tr)]
        if (dz, dy) == (0, 0):
            own = [
                pltpu.make_async_copy(src_v, got_v.at[k], load_sem.at[3]),
                pltpu.make_async_copy(src_t, got_t.at[k], load_sem.at[4]),
            ]
        else:
            first += [
                send(src_v, got_v.at[k], s1.at[k], r1.at[k], at(dz, dy)),
                send(src_t, got_t.at[k], s1.at[k + PIECES], r1.at[k + PIECES], at(dz, dy)),
            ]
    for c in first + own:
        c.start()

    ident[...] = jnp.zeros_like(ident)
    shift_x[...] = jnp.zeros_like(shift_x)
    shift_e[...] = jnp.zeros_like(shift_e)
    shift_p[...] = jnp.zeros_like(shift_p)
    for c in own:
        c.wait()
    for i in range(3):
        pl.semaphore_wait(relay.at[i], 1)
    pl.semaphore_signal(relay.at[3], inc=1, device_id=at(0, T), device_id_type=MESH)
    for c in first:
        c.wait_recv()

    lots = steps
    second, third = [], []
    rest = 2 * vr
    unit = blocks_step * vr // nfar
    units = rest // unit

    def place_of(lot, f):
        return lot * blocks_step // 2 + f // units, pl.ds(pl.multiple_of(f % units * unit, unit), unit)

    def where_is(slot):
        root = slot // 2
        az = (z - root // NY + nz + 1) % nz
        ay = (y - root % NY + NY + 1) % NY
        here = jnp.logical_and(az < T, ay < T)
        return here, jnp.minimum(az, T - 1) * T + jnp.minimum(ay, T - 1), slot % 2

    for lot in range(lots):
        sends = []
        for b in range(lot * blocks_step, (lot + 1) * blocks_step):
            here, k, half = where_is(slots[0, b // blocks_step, b % blocks_step])
            mine[b // 2, (b % 2) * vr : (b % 2 + 1) * vr] = jnp.where(here, got_v[k, half], 0.0)
        if lot == 0:
            for q in range(blocks // 2):
                one = slots[0, 2 * q // blocks_step, 2 * q % blocks_step]
                two = slots[0, (2 * q + 1) // blocks_step, (2 * q + 1) % blocks_step]
                here, k, half = where_is(jnp.where(p_me < PIECES // 2, one, two))
                mine[q, rest : rest + tr] = jnp.where(here, got_t[k, half], 0.0)
        for a, b in fars:
            k = a * nyh + b
            dest = ((zh + a) % nzh) * nyh + (yh + b) % nyh
            q, part = place_of(lot, dest)
            j = lot * nfar + k
            dev = at(T * a, T * b)
            sends.append(send(mine.at[q, part], far.at[lot, k], s2.at[j], r2.at[j], dev))
            if lot == 0:
                src = mine.at[dest, rest : rest + tr]
                sends.append(send(src, far_t.at[k], st.at[k], rt.at[k], dev))
        for i, c in enumerate(sends):
            if lot == 0 and i == 2 * (nfar - 2):
                pl.semaphore_wait(relay.at[3], 1)
            c.start()
        second.append(sends)

    for lot in range(lots):
        me, part = place_of(lot, f_me)
        total = mine[me, part]
        for c in second[lot]:
            c.wait_recv()
        for k in range(1, nfar):
            total = total + far[lot, k]
        full[me, zl, yl, part] = total
        shards = [full.at[me, zl, yl, part]]
        if lot == 0:
            total = mine[f_me, rest : rest + tr]
            for k in range(1, nfar):
                total = total + far_t[k]
            full[f_me, zl, yl, rest : rest + tr] = total
            shards.append(full.at[f_me, zl, yl, rest : rest + tr])
        sends = []
        for a, b in fars:
            k = a * nyh + b
            j = lot * nfar + k
            for i, shard in enumerate(shards):
                ssem, rsem = (s3.at[j], r3.at[j]) if i == 0 else (st.at[nfar + k], rt.at[nfar + k])
                sends.append(send(shard, shard, ssem, rsem, at(T * a, T * b)))
        for c in sends:
            c.start()
        third.append(sends)

    pairs = blocks_step // 2

    def near(step, turn):
        sends = []
        s, r = (s4, r4) if turn == 0 else (s5, r5)
        for i, (dz, dy) in enumerate(NEAR):
            along_z = dy == 0
            lo, n = step * pairs + (0 if along_z == (turn == 0) else pairs // 2), pairs // 2
            rows = slice(0, rest + tr)
            if abs(dz + dy) == 2:
                rows = slice(0, vr) if (dz + dy > 0) == (step % 2 == 0) else slice(vr, rest + tr)
            if turn == 0:
                ref = full.at[pl.ds(lo, n), zl, yl, rows]
            elif along_z:
                ref = full.at[pl.ds(lo, n), zl, :, rows]
            else:
                ref = full.at[pl.ds(lo, n), :, yl, rows]
            j = step * len(NEAR) + i
            sends.append(send(ref, ref, s.at[j], r.at[j], at(dz, dy)))
        return sends

    fourth = [near(s, 0) for s in range(steps)]
    fifth = [near(s, 1) for s in range(steps)]
    for lot in range(lots):
        for c in third[lot]:
            c.wait_recv()
        for s in range(lot * steps // lots, (lot + 1) * steps // lots):
            for c in fourth[s]:
                c.start()
    load.wait()
    for s in range(steps):
        for c in fourth[s]:
            c.wait_recv()
        for c in fifth[s]:
            c.start()

    rows = out.shape[0]
    edge = head.shape[2]
    tall = 2 * edge
    has_below = group < groups - 1
    eye = (
        lax.broadcasted_iota(jnp.int32, (edge, edge), 0) == lax.broadcasted_iota(jnp.int32, (edge, edge), 1)
    ).astype(F32)
    halo = []

    def block(b):
        h = b % 2
        basis = full[b // 2, :, :, h * vr : (h + 1) * vr].reshape(tall, edge)
        factor = unpack(full[b // 2, h * T // 2 : (h + 1) * T // 2, :, rest : rest + tr].reshape(edge // 2, edge))
        return split(basis.T), split(factor), split(basis)

    def apply(ops, x):
        w = mul(ops[0], split(x))
        return mul(ops[2], split(mul(ops[1], split(w))))

    ident[0:edge] = eye

    def window(target, shifts, starts, start, reach, count):
        x = target[pl.ds(start, count)]
        for shift, o in zip(shifts, starts):
            x = x - shift[pl.ds(reach - o + start, count)]
        return x

    head[0, 0] = out[0:edge]
    up = send(head.at[0, 0], beneath.at[0, 0], sh.at[0], rh.at[0], row(-1))
    up.start()
    ups, dns = [up], []
    for c in first:
        c.wait_send()
    for cs in second + third:
        for c in cs:
            c.wait_send()
    for s in range(steps):
        for c in fourth[s] + (fifth[s - 1] if s > 0 else []):
            c.wait_send()
        for c in fifth[s]:
            c.wait_recv()
        at_x, at_e, at_p, parts = [], [], [], []
        for j in range(inner):
            ops = block(s * blocks_step + j)
            o = offs[0, s, j]
            oe, op = jnp.minimum(o, REACH), jnp.minimum(o, FAR_REACH)
            x = [
                window(out, [shift_x.at[i] for i in range(j)], at_x, o, rows - tall, tall),
                window(ident, [shift_e.at[i] for i in range(j)], at_e, oe, REACH, tall),
            ]
            if s > 0:
                x.append(window(pending, [shift_p.at[i] for i in range(j)], at_p, op, FAR_REACH, tall))
            d = apply(ops, jnp.concatenate(x, 1))
            shift_x[j, rows - tall : rows] = d[:, :edge]
            shift_e[j, REACH : REACH + tall] = d[:, edge : 2 * edge]
            if s > 0:
                shift_p[j, FAR_REACH : FAR_REACH + tall] = d[:, 2 * edge :]
            at_x, at_e, at_p = at_x + [o], at_e + [oe], at_p + [op]
        all_x, all_e, all_p = ([f.at[i] for i in range(inner)] for f in (shift_x, shift_e, shift_p))
        ops = block(s * blocks_step + inner)
        tail = window(out, all_x, at_x, rows - edge, rows - tall, edge)
        ups[s].wait_recv()
        under = beneath[s, 0]
        if s > 0:
            under = under - mul(split(beneath[s, 1]), split(down[s - 1]))
        d = jnp.where(has_below, apply(ops, jnp.concatenate([tail, under], 0)), 0.0)
        down[s] = d[edge:]
        dn = send(down.at[s], delta.at[s], sh.at[steps + s], rh.at[steps + s], row(1))
        dn.start()
        dns.append(dn)
        for i in range(0, rows - edge, edge):
            out[i : i + edge] = window(out, all_x, at_x, i, rows - tall, edge)
        out[rows - edge :] = tail - d[:edge]
        if s > 0:
            carry = split(window(pending, all_p, at_p, 0, FAR_REACH, FAR_REACH))
            dns[s - 1].wait_recv()
            out[0:FAR_REACH] -= mul(carry, split(delta[s - 1]))
        for i in range(0, REACH, edge):
            pending[i : i + edge] = window(ident, all_e, at_e, i, REACH, edge)
        if s == 0:
            pending[REACH:] = jnp.zeros((pending.shape[0] - REACH, edge), F32)
        if s < steps - 1:
            head[s + 1, 0] = out[0:edge]
            head[s + 1, 1] = pending[0:edge]
            up = send(head.at[s + 1], beneath.at[s + 1], sh.at[s + 1], rh.at[s + 1], row(-1))
            up.start()
            ups.append(up)
    carry = split(pending[0:REACH])
    dns[steps - 1].wait_recv()
    out[0:REACH] -= mul(carry, split(delta[steps - 1]))
    halo = ups + dns

    for c in fifth[steps - 1] + halo:
        c.wait_send()


def solution(mesh):
    groups = mesh.shape["row"]
    nz = mesh.shape["col"] // NY

    def per_device(vectors, reflectors, wy_factors, block_slots, offsets):
        steps, inner = offsets.shape[1:]
        blocks = steps * (inner + 1)
        rows, width = vectors.shape
        hold, tall, edge = reflectors.shape[1:]
        vr, tr = tall // PIECES, edge // PIECES
        nfar = (nz // T) * (NY // T)
        dma = pltpu.SemaphoreType.DMA
        vmem = pltpu.VMEM
        return pl.pallas_call(
            functools.partial(kernel, nz, groups, steps, inner),
            out_shape=jax.ShapeDtypeStruct((rows, width), F32),
            in_specs=[pl.BlockSpec(memory_space=pltpu.SMEM)] * 2 + [pl.BlockSpec(memory_space=pl.ANY)] * 3,
            out_specs=pl.BlockSpec(memory_space=pltpu.VMEM),
            scratch_shapes=[
                vmem((hold, tall, edge), F32),
                vmem((hold, edge, edge), F32),
                vmem((PIECES, hold, vr, edge), F32),
                vmem((PIECES, hold, tr, edge), F32),
                vmem((blocks // 2, 2 * vr + tr, edge), F32),
                vmem((steps, nfar, (inner + 1) * vr // nfar, edge), F32),
                vmem((nfar, tr, edge), F32),
                vmem((blocks // 2, T, T, 2 * vr + tr, edge), F32),
                vmem((REACH + tall, width), F32),
                vmem((FAR_REACH + tall, width), F32),
                vmem((inner, 2 * rows - tall, width), F32),
                vmem((inner, 2 * REACH + tall, width), F32),
                vmem((inner, 2 * FAR_REACH + tall, width), F32),
                vmem((steps, 2, edge, width), F32),
                vmem((steps, 2, edge, width), F32),
                vmem((steps, edge, width), F32),
                vmem((steps, edge, width), F32),
                dma((5,)),
                pltpu.SemaphoreType.REGULAR((4,)),
                dma((2 * PIECES,)), dma((2 * PIECES,)),
                dma((steps * nfar,)), dma((steps * nfar,)),
                dma((steps * nfar,)), dma((steps * nfar,)),
                dma((2 * nfar,)), dma((2 * nfar,)),
                dma((steps * len(NEAR),)), dma((steps * len(NEAR),)),
                dma((steps * len(NEAR),)), dma((steps * len(NEAR),)),
                dma((2 * steps,)), dma((2 * steps,)),
            ],
            compiler_params=pltpu.CompilerParams(
                collective_id=0, has_side_effects=True, vmem_limit_bytes=40 * 1024 * 1024
            ),
        )(block_slots, offsets, vectors, reflectors, wy_factors)

    in_specs = (
        P("row", "col"),
        P("row", "col", None, None),
        P("row", "col", None, None),
        P("row", None, None),
        P("row", None, None),
    )
    return jax.shard_map(per_device, mesh=mesh, in_specs=in_specs, out_specs=P("row", "col"), check_vma=False)
```
